256 devices in a mesh: gx: 8 (over x, core), gy: 4 (over y), band: 8 (over z).
Axes of the slice: x: 4, y: 4, z: 8, core: 2. Of those that a mesh axis runs over, the one named last changes fastest.
Arguments:
- orbitals: float32 [160, 48, 32, 128], P('band', 'gx', 'gy'), may hold values from -6 to 6
- potential: float32 [48, 32, 128], P('gx', 'gy'), may hold values from -1 to 1
Outputs:
- filtered: float32 [160, 48, 32, 128], P('band', 'gx', 'gy')
- correlation: float32 [160, 160], P('band')
- projected: float32 [160, 160], P('band')
The draws below stay inside these ranges and needn't reach their ends.
All inputs are finite; a program needn't handle non-finite values.
Results may differ from the reference program's by a relative error of at most 0.000051.
Values sent between devices are 32-bit elements; how exact they have to be, the bound alone decides.
A program may use at most 64 MiB of HBM per device.

```python
import jax
import jax.numpy as jnp
from jax import lax

M = 160
NZ = 128
NX = 48
NY = 32


def shard_levels(key, extent, pieces, least, top_value):
    def one(dim, blocks):
        heights = jax.random.uniform(jax.random.fold_in(jax.random.fold_in(key, 6), dim), (blocks,), jnp.float32, least / len(pieces), top_value / len(pieces))
        return jnp.repeat(jnp.exp(heights), extent[dim] // blocks).reshape((-1,) + (1,) * (len(extent) - dim - 1))

    level = one(*pieces[0])
    for cut in pieces[1:]:
        level = level * one(*cut)
    return level


def scatter_about(key, dims, deviation, bound, pieces=(), dtype=jnp.bfloat16):
    array = jax.random.normal(key, dims, jnp.float32) * deviation
    if len(pieces) > 0:
        array = shard_levels(key, dims, pieces, -0.22, 0.18) * array
    return jnp.clip(array, min=-bound, max=bound).astype(dtype)


def setup_inputs(seed: int = 0) -> dict:
    seeds = jax.random.split(jax.random.key(seed), 3)
    return {
        "orbitals": scatter_about(seeds[0], (M, NX, NY, NZ), 1.0, 6.0, ((0, 8), (1, 8), (2, 4)), jnp.float32),
        "potential": jnp.clip(jax.random.uniform(seeds[1], (NX, NY, NZ), jnp.float32, -1.0, 1.0) * shard_levels(seeds[1], (NX, NY, NZ), ((0, 8), (1, 4)), -0.4, 0.0), -1.0, 1.0),
    }


stencil_weights = (-5369.0 / 1800.0, 12.0 / 7.0, -15.0 / 56.0, 10.0 / 189.0, -1.0 / 112.0, 2.0 / 1925.0, -1.0 / 16632.0)
center_level = 7.5
half_width = 4.5


def hamiltonian(orbital_field, potential):
    depth = orbital_field.shape[3]
    depth_pad = jnp.pad(orbital_field, ((0, 0), (0, 0), (0, 0), (6, 6)))
    laplace = 3.0 * stencil_weights[0] * orbital_field
    for offset in range(1, 7):
        weight = stencil_weights[offset]
        laplace = laplace + weight * (jnp.roll(orbital_field, offset, 1) + jnp.roll(orbital_field, -offset, 1))
        laplace = laplace + weight * (jnp.roll(orbital_field, offset, 2) + jnp.roll(orbital_field, -offset, 2))
        laplace = laplace + weight * (depth_pad[:, :, :, 6 + offset:6 + offset + depth] + depth_pad[:, :, :, 6 - offset:6 - offset + depth])
    return -0.5 * laplace + potential[None] * orbital_field


def reference(orbitals, potential):
    first = (hamiltonian(orbitals, potential) - center_level * orbitals) / half_width
    second = (2.0 / half_width) * (hamiltonian(first, potential) - center_level * first) - orbitals
    filtered = (2.0 / half_width) * (hamiltonian(second, potential) - center_level * second) - first
    image = hamiltonian(filtered, potential)
    flat_filtered = filtered.reshape(M, -1)
    flat_image = image.reshape(M, -1)
    scale = 1.0 / (NX * NY * NZ)
    correlation = jnp.dot(flat_filtered, flat_filtered.T, precision=lax.Precision.HIGHEST, preferred_element_type=jnp.float32) * scale
    projected = jnp.dot(flat_image, flat_filtered.T, precision=lax.Precision.HIGHEST, preferred_element_type=jnp.float32) * scale
    return filtered, correlation, projected
```

```python
import functools

import jax
import jax.numpy as jnp
from jax import lax
from jax.experimental import pallas as pl
from jax.experimental.pallas import tpu as pltpu
from jax.sharding import PartitionSpec as P

stencil_weights = (
    -5369.0 / 1800.0,
    12.0 / 7.0,
    -15.0 / 56.0,
    10.0 / 189.0,
    -1.0 / 112.0,
    2.0 / 1925.0,
    -1.0 / 16632.0,
)
center_level = 7.5
half_width = 4.5

MESH = pl.DeviceIdType.MESH
F32 = jnp.float32
PART = 4


def kernel(
    dims,
    scale,
    v_ref,
    pot_ref,
    filt_ref,
    corr_ref,
    proj_ref,
    own,
    tall,
    xlo,
    xhi,
    diag,
    stage,
    gather,
    rows_out,
    rows_in,
    gx_in,
    gy_in,
    load_sem,
    halo_send,
    halo_recv,
    z_send,
    z_recv,
    r_send,
    r_recv,
    s_send,
    s_recv,
):
    ngx, ngy, nb = dims
    norb, wx, wy, nz = v_ref.shape
    chunks = norb // PART
    gx, gy, band = lax.axis_index("gx"), lax.axis_index("gy"), lax.axis_index("band")

    load = pltpu.make_async_copy(v_ref, own.at[0], load_sem)
    load.start()

    barrier = pltpu.get_barrier_semaphore()
    for d in range(1, ngx):
        pl.semaphore_signal(barrier, 1, device_id={"gx": lax.rem(gx + d, ngx)}, device_id_type=MESH)
    for d in range(1, ngy):
        pl.semaphore_signal(barrier, 1, device_id={"gy": lax.rem(gy + d, ngy)}, device_id_type=MESH)
    for d in range(1, nb):
        pl.semaphore_signal(barrier, 1, device_id={"band": lax.rem(band + d, nb)}, device_id_type=MESH)

    diag[...] = (pot_ref[...] - 1.5 * stencil_weights[0] - center_level) * (1.0 / half_width)
    taps = [0.0] + [-0.5 * w / half_width for w in stencil_weights[1:]]
    lane = lax.broadcasted_iota(jnp.int32, (wy, nz), 1)

    load.wait()

    def fill(n, carry):
        for x in range(wx):
            tall[0, n, x, 8:16] = own[0, n, x]
        return carry

    lax.fori_loop(0, norb, fill, 0)
    pl.semaphore_wait(barrier, ngx + ngy + nb - 3)

    sides = (
        {"gx": lax.rem(gx + 1, ngx)},
        {"gx": lax.rem(gx + ngx - 1, ngx)},
        {"gy": lax.rem(gy + 1, ngy)},
        {"gy": lax.rem(gy + ngy - 1, ngy)},
    )

    def halo_copy(level, start, count, sem_at, side):
        group = pl.ds(start, count)
        if side == 0:
            src, dst = own.at[level, group], xlo.at[level, group]
        elif side == 1:
            src, dst = own.at[level, group], xhi.at[level, group]
        elif side == 2:
            src, dst = own.at[level, group, :, 2:8], tall.at[level, group, :, 2:8]
        else:
            src, dst = own.at[level, group, :, 0:6], tall.at[level, group, :, 16:22]
        return pltpu.make_async_remote_copy(
            src_ref=src,
            dst_ref=dst,
            send_sem=halo_send.at[level, side],
            recv_sem=halo_recv.at[level, sem_at, side],
            device_id=sides[side],
            device_id_type=MESH,
        )

    def halo_start(level, c):
        for side in (2, 3, 0, 1):
            halo_copy(level, c * PART, PART, c, side).start()

    def halo_wait(level, c):
        for side in (0, 1, 2, 3):
            halo_copy(level, c * PART, PART, c, side).wait_recv()

    def base(level, n):
        line = (
            [xlo[level, n, x] for x in range(wx)]
            + [own[level, n, x] for x in range(wx)]
            + [xhi[level, n, x] for x in range(wx)]
        )
        out = []
        for x in range(wx):
            v = line[wx + x]
            total = diag[x] * v
            for k in range(1, 7):
                near = line[wx + x + k] + line[wx + x - k]
                near += tall[level, n, x, 8 + k : 16 + k] + tall[level, n, x, 8 - k : 16 - k]
                near += jnp.where(lane < nz - k, pltpu.roll(v, nz - k, 1), 0.0)
                near += jnp.where(lane >= k, pltpu.roll(v, k, 1), 0.0)
                total += taps[k] * near
            out.append(total)
        return out

    def z_start(which, c):
        for d in range(1, nb):
            peer = lax.rem(band + d, nb)
            pltpu.make_async_remote_copy(
                src_ref=stage.at[which, c, peer],
                dst_ref=gather.at[which, pl.ds(pl.multiple_of(band * (norb * wx) + c * (PART * wx), 8), PART * wx)],
                send_sem=z_send.at[which],
                recv_sem=z_recv.at[which],
                device_id={"band": peer},
                device_id_type=MESH,
            ).start()

    def spread(which, c, value):
        turned = jnp.swapaxes(value, 0, 1)
        stage[which, c] = turned
        mine = pl.ds(pl.multiple_of(band * (norb * wx) + c * (PART * wx), 8), PART * wx)
        gather[which, mine] = stage[which, c, band]

    def first_sends(c, carry):
        halo_start(0, c)
        return carry

    lax.fori_loop(0, chunks, first_sends, 0)

    def step(level, c):
        halo_wait(level, c)

        def one(i, carry):
            n = c * PART + i
            for x, value in enumerate(base(level, n)):
                if level > 0:
                    value = 2.0 * value - own[level - 1, n, x]
                own[level + 1, n, x] = value
                tall[level + 1, n, x, 8:16] = value
            return carry

        lax.fori_loop(0, PART, one, 0)
        halo_start(level + 1, c)
        if level == 2:
            block = own[3, pl.ds(c * PART, PART)].reshape(PART * wx, wy, nz)
            spread(0, c, block)
            z_start(0, c)

    for level in range(3):
        def body(c, carry, level=level):
            step(level, c)
            return carry

        lax.fori_loop(0, chunks, body, 0)

    save = pltpu.make_async_copy(own.at[3], filt_ref, load_sem)
    save.start()

    def last(c, carry):
        halo_wait(3, c)

        def one(i, carry):
            n = c * PART + i
            for x, value in enumerate(base(3, n)):
                own[4, n, x] = half_width * value + center_level * own[3, n, x]
            return carry

        lax.fori_loop(0, PART, one, 0)
        block = own[4, pl.ds(c * PART, PART)].reshape(PART * wx, wy, nz)
        spread(1, c, block)
        z_start(1, c)
        return carry

    lax.fori_loop(0, chunks, last, 0)

    share = norb * wx * (nb - 1)

    def z_done(which):
        return pltpu.make_async_remote_copy(
            src_ref=gather.at[which, pl.ds(0, share)],
            dst_ref=gather.at[which, pl.ds(0, share)],
            send_sem=z_send.at[which],
            recv_sem=z_recv.at[which],
            device_id={"band": lax.rem(band + 1, nb)},
            device_id_type=MESH,
        )

    total_orbs = norb * nb

    def operand(which):
        return jnp.concatenate(
            [gather[which, pl.ds(x, total_orbs, stride=wx), :] for x in range(wx)], axis=1
        )

    def product(a, b):
        return lax.dot_general(
            a, b, (((1,), (1,)), ((), ())), precision=lax.Precision.HIGHEST, preferred_element_type=F32
        )

    def rows_copy(which, peer):
        return pltpu.make_async_remote_copy(
            src_ref=rows_out.at[which, peer],
            dst_ref=rows_in.at[which, band],
            send_sem=r_send.at[which],
            recv_sem=r_recv.at[which],
            device_id={"band": peer},
            device_id_type=MESH,
        )

    def rows_done(which):
        return pltpu.make_async_remote_copy(
            src_ref=rows_in.at[which, pl.ds(0, nb - 1)],
            dst_ref=rows_in.at[which, pl.ds(0, nb - 1)],
            send_sem=r_send.at[which],
            recv_sem=r_recv.at[which],
            device_id={"band": lax.rem(band + 1, nb)},
            device_id_type=MESH,
        )

    def scatter(which, value):
        rows_out[which] = value.reshape(nb, norb, total_orbs)
        rows_in[which, band] = rows_out[which, band]
        for d in range(1, nb):
            rows_copy(which, lax.rem(band + d, nb)).start()

    z_done(0).wait_recv()
    scatter(0, product(operand(0), operand(0)))
    z_done(1).wait_recv()
    scatter(1, product(operand(1), operand(0)))

    def ordered(ref, count):
        value = ref[0]
        for i in range(1, count):
            value = value + ref[i]
        return value

    for which in range(2):
        rows_done(which).wait_recv()
        value = rows_in[which, 0]
        for i in range(1, nb):
            value = value + rows_in[which, i]
        gx_in[gx, which] = value

    def gx_copy(peer):
        return pltpu.make_async_remote_copy(
            src_ref=gx_in.at[gx],
            dst_ref=gx_in.at[gx],
            send_sem=s_send.at[0],
            recv_sem=s_recv.at[0],
            device_id={"gx": peer},
            device_id_type=MESH,
        )

    for d in range(1, ngx):
        gx_copy(lax.rem(gx + d, ngx)).start()
    gx_done = pltpu.make_async_remote_copy(
        src_ref=gx_in.at[pl.ds(0, ngx - 1)],
        dst_ref=gx_in.at[pl.ds(0, ngx - 1)],
        send_sem=s_send.at[0],
        recv_sem=s_recv.at[0],
        device_id={"gx": lax.rem(gx + 1, ngx)},
        device_id_type=MESH,
    )
    gx_done.wait_recv()
    gy_in[gy] = ordered(gx_in, ngx)

    for d in range(1, ngy):
        pltpu.make_async_remote_copy(
            src_ref=gy_in.at[gy],
            dst_ref=gy_in.at[gy],
            send_sem=s_send.at[1],
            recv_sem=s_recv.at[1],
            device_id={"gy": lax.rem(gy + d, ngy)},
            device_id_type=MESH,
        ).start()
    gy_done = pltpu.make_async_remote_copy(
        src_ref=gy_in.at[pl.ds(0, ngy - 1)],
        dst_ref=gy_in.at[pl.ds(0, ngy - 1)],
        send_sem=s_send.at[1],
        recv_sem=s_recv.at[1],
        device_id={"gy": lax.rem(gy + 1, ngy)},
        device_id_type=MESH,
    )
    gy_done.wait_recv()
    sums = ordered(gy_in, ngy) * scale
    corr_ref[...] = sums[0]
    proj_ref[...] = sums[1]

    for level in range(4):
        for side in range(4):
            halo_copy(level, 0, norb, 0, side).wait_send()
    for which in range(2):
        z_done(which).wait_send()
        rows_done(which).wait_send()
    gx_done.wait_send()
    gy_done.wait_send()
    save.wait()


def body(orbitals, potential):
    norb, wx, wy, nz = orbitals.shape
    ngx, ngy, nb = lax.axis_size("gx"), lax.axis_size("gy"), lax.axis_size("band")
    total = norb * nb
    chunks = norb // PART
    scale = 1.0 / (wx * wy * nz * ngx * ngy)
    block = (norb, wx, wy, nz)
    vmem = pl.BlockSpec(memory_space=pltpu.VMEM)
    hbm = pl.BlockSpec(memory_space=pl.ANY)
    return pl.pallas_call(
        functools.partial(kernel, (ngx, ngy, nb), scale),
        out_shape=(
            jax.ShapeDtypeStruct(block, F32),
            jax.ShapeDtypeStruct((norb, total), F32),
            jax.ShapeDtypeStruct((norb, total), F32),
        ),
        in_specs=[hbm, vmem],
        out_specs=(hbm, vmem, vmem),
        scratch_shapes=[
            pltpu.VMEM((5,) + block, F32),
            pltpu.VMEM((4, norb, wx, 24, nz), F32),
            pltpu.VMEM((4,) + block, F32),
            pltpu.VMEM((4,) + block, F32),
            pltpu.VMEM((wx, wy, nz), F32),
            pltpu.VMEM((2, chunks, nb, PART * wx, nz), F32),
            pltpu.VMEM((2, total * wx, nz), F32),
            pltpu.VMEM((2, nb, norb, total), F32),
            pltpu.VMEM((2, nb, norb, total), F32),
            pltpu.VMEM((ngx, 2, norb, total), F32),
            pltpu.VMEM((ngy, 2, norb, total), F32),
            pltpu.SemaphoreType.DMA,
            pltpu.SemaphoreType.DMA((4, 4)),
            pltpu.SemaphoreType.DMA((4, chunks, 4)),
            pltpu.SemaphoreType.DMA((2,)),
            pltpu.SemaphoreType.DMA((2,)),
            pltpu.SemaphoreType.DMA((2,)),
            pltpu.SemaphoreType.DMA((2,)),
            pltpu.SemaphoreType.DMA((2,)),
            pltpu.SemaphoreType.DMA((2,)),
        ],
        compiler_params=pltpu.CompilerParams(
            collective_id=0, has_side_effects=True, vmem_limit_bytes=48 * 1024 * 1024
        ),
        cost_estimate=pl.CostEstimate(flops=200_000_000, bytes_accessed=2_000_000, transcendentals=0),
    )(orbitals, potential)


def solution(mesh):
    in_specs = (P("band", "gx", "gy", None), P("gx", "gy", None))
    out_specs = (P("band", "gx", "gy", None), P("band", None), P("band", None))
    return jax.shard_map(body, mesh=mesh, in_specs=in_specs, out_specs=out_specs, check_vma=False)
```

```python
import functools

import jax
import jax.numpy as jnp
from jax import lax
from jax.experimental import pallas as pl
from jax.experimental.pallas import tpu as pltpu
from jax.sharding import PartitionSpec as P

stencil_weights = (
    -5369.0 / 1800.0,
    12.0 / 7.0,
    -15.0 / 56.0,
    10.0 / 189.0,
    -1.0 / 112.0,
    2.0 / 1925.0,
    -1.0 / 16632.0,
)
center_level = 7.5
half_width = 4.5

MESH = pl.DeviceIdType.MESH
F32 = jnp.float32
PART = 4


def kernel(
    dims,
    scale,
    v_ref,
    pot_ref,
    filt_ref,
    corr_ref,
    proj_ref,
    own,
    tall,
    xlo,
    xhi,
    diag,
    shift_w,
    stage,
    gather,
    tail,
    rows_out,
    rows_in,
    gx_in,
    gy_in,
    load_sem,
    ready,
    halo_send,
    halo_recv,
    z_send,
    z_recv,
    r_send,
    r_recv,
    s_send,
    s_recv,
):
    ngx, ngy, nb = dims
    norb, wx, wy, nz = own.shape[1:]
    chunks = norb // PART
    total_orbs = norb * nb
    half_x, half_y = wx // 2, wy // 2
    gx, gy, band = lax.axis_index("gx"), lax.axis_index("gy"), lax.axis_index("band")

    load = pltpu.make_async_copy(v_ref, own.at[0], load_sem.at[0])
    load.start()
    load_pot = pltpu.make_async_copy(pot_ref, diag, load_sem.at[1])
    load_pot.start()

    sides = (
        {"gx": lax.rem(gx + 1, ngx)},
        {"gx": lax.rem(gx + ngx - 1, ngx)},
        {"gy": lax.rem(gy + 1, ngy)},
        {"gy": lax.rem(gy + ngy - 1, ngy)},
        {"band": lax.rem(band + 1, nb)},
        {"band": lax.rem(band + nb - 1, nb)},
    )

    def clear(n, carry):
        for x in range(wx):
            xlo[3, n, x, 0:half_y] = jnp.zeros((half_y, nz), F32)
            xhi[3, n, x, half_y:wy] = jnp.zeros((wy - half_y, nz), F32)
            if x < half_x:
                tall[3, n, x, 0:8] = jnp.zeros((8, nz), F32)
            else:
                tall[3, n, x, 16:24] = jnp.zeros((8, nz), F32)
        return carry

    lax.fori_loop(0, norb, clear, 0)

    barrier = pltpu.get_barrier_semaphore()
    for peer in sides:
        pl.semaphore_signal(barrier, 1, device_id=peer, device_id_type=MESH)

    taps = [0.0] + [-0.5 * w / half_width for w in stencil_weights[1:]]
    lane = lax.broadcasted_iota(jnp.int32, (wy, nz), 1)

    spots = (
        [(0, j) for j in (-2, -1, 1, 2)]
        + [(5, j) for j in (-2, -1, 0, 1)]
        + [(-5, j) for j in (-1, 0, 1, 2)]
    )
    for i, (far, j) in enumerate(spots):
        where = lane + far
        where = jnp.where(where >= nz, where - nz, jnp.where(where < 0, where + nz, where))
        source = where - (far + j)
        inside = jnp.logical_and(source >= 0, source < nz)
        shift_w[i] = jnp.where(inside, taps[abs(far + j)], 0.0)

    tail[...] = jnp.zeros_like(tail)
    load.wait()
    load_pot.wait()
    diag[...] = (diag[...] - 1.5 * stencil_weights[0] - center_level) * (1.0 / half_width)

    def fill(n, carry):
        for x in range(wx):
            tall[0, n, x, 8:16] = own[0, n, x]
        return carry

    lax.fori_loop(0, norb, fill, 0)
    pl.semaphore_wait(barrier, 6)

    def relay(turn):
        for peer in sides:
            pl.semaphore_signal(ready.at[turn], 1, device_id=peer, device_id_type=MESH)

    def heard(turn):
        pl.semaphore_wait(ready.at[turn], 6)

    def halo_copy(level, start, count, sem_at, side):
        group = pl.ds(start, count)
        if level < 3:
            src = (
                own.at[level, group],
                own.at[level, group],
                own.at[level, group, :, 2:8],
                own.at[level, group, :, 0:6],
            )[side]
            dst = (
                xlo.at[level, group],
                xhi.at[level, group],
                tall.at[level, group, :, 2:8],
                tall.at[level, group, :, 16:22],
            )[side]
        else:
            src = (
                own.at[level, group, :, half_y:wy],
                own.at[level, group, :, 0:half_y],
                own.at[level, group, half_x:wx, 2:8],
                own.at[level, group, 0:half_x, 0:6],
            )[side]
            dst = (
                xlo.at[level, group, :, half_y:wy],
                xhi.at[level, group, :, 0:half_y],
                tall.at[level, group, half_x:wx, 2:8],
                tall.at[level, group, 0:half_x, 16:22],
            )[side]
        return pltpu.make_async_remote_copy(
            src_ref=src,
            dst_ref=dst,
            send_sem=halo_send.at[level, side],
            recv_sem=halo_recv.at[level, sem_at, side],
            device_id=sides[side],
            device_id_type=MESH,
        )

    def halo_start(level, c):
        for side in (2, 3, 0, 1):
            halo_copy(level, c * PART, PART, c, side).start()

    def halo_wait(level, c):
        for side in (0, 1, 2, 3):
            halo_copy(level, c * PART, PART, c, side).wait_recv()

    def base(level, n):
        inner = [own[level, n, x] for x in range(wx)]
        if level == 3:
            inner = [0.5 * v for v in inner]
        line = [xlo[level, n, x] for x in range(wx)] + inner + [xhi[level, n, x] for x in range(wx)]
        out = []
        for x in range(wx):
            v = inner[x]
            total = diag[x] * v
            for k in range(1, 7):
                near = line[wx + x + k] + line[wx + x - k]
                near += tall[level, n, x, 8 + k : 16 + k] + tall[level, n, x, 8 - k : 16 - k]
                total += taps[k] * near
            rolled = {0: v}
            for j in (-2, -1, 1, 2):
                rolled[j] = pltpu.roll(v, j % nz, 1)
            parts = {0: None, 5: None, -5: None}
            for i, (far, j) in enumerate(spots):
                term = shift_w[i] * rolled[j]
                parts[far] = term if parts[far] is None else parts[far] + term
            total += parts[0]
            total += pltpu.roll(parts[5], 5, 1) + pltpu.roll(parts[-5], nz - 5, 1)
            out.append(total)
        return out

    def z_rows(c):
        return pl.ds(pl.multiple_of(band * (norb * wx) + c * (PART * wx), 8), PART * wx)

    def spread(which, c, value):
        stage[which, c] = jnp.swapaxes(value, 0, 1)
        gather[which, z_rows(c)] = stage[which, c, band]
        for d in (1, 2, 3, 4, -1, -2, -3):
            peer = lax.rem(band + d + nb, nb)
            pltpu.make_async_remote_copy(
                src_ref=stage.at[which, c, peer],
                dst_ref=gather.at[which, z_rows(c)],
                send_sem=z_send.at[which],
                recv_sem=z_recv.at[which],
                device_id={"band": peer},
                device_id_type=MESH,
            ).start()

    def step(level, c):
        halo_wait(level, c)

        def one(i, carry):
            n = c * PART + i
            for x, value in enumerate(base(level, n)):
                if level in (1, 2):
                    value = 2.0 * value - own[level - 1, n, x]
                elif level == 3:
                    value = half_width * value + (0.5 * center_level) * own[3, n, x]
                own[level + 1, n, x] = value
                if level < 3:
                    tall[level + 1, n, x, 8:16] = 0.5 * value if level == 2 else value
            return carry

        lax.fori_loop(0, PART, one, 0)
        if level < 3:
            halo_start(level + 1, c)
        if level >= 2:
            spread(level - 2, c, own[level + 1, pl.ds(c * PART, PART)].reshape(PART * wx, wy, nz))

    def run(level, first, end):
        def body(c, carry):
            if level < 0:
                halo_start(0, c)
            else:
                step(level, c)
            return carry

        lax.fori_loop(first, end, body, 0)

    cut = (chunks + 1) // 2
    run(-1, 0, cut)
    relay(0)
    heard(0)
    relay(1)
    run(0, 0, cut)
    heard(1)
    relay(2)
    run(1, 0, cut)
    run(-1, cut, chunks)
    heard(2)
    run(2, 0, cut)
    run(0, cut, chunks)
    run(3, 0, cut)
    run(1, cut, chunks)
    run(2, cut, chunks)
    save = pltpu.make_async_copy(own.at[3], filt_ref, load_sem.at[0])
    save.start()
    run(3, cut, chunks)

    def all_of(ref, count, send, recv, peer):
        part = ref.at[pl.ds(0, count)]
        return pltpu.make_async_remote_copy(
            src_ref=part, dst_ref=part, send_sem=send, recv_sem=recv, device_id=peer, device_id_type=MESH
        )

    def z_done(which):
        return all_of(gather.at[which], norb * wx * (nb - 1), z_send.at[which], z_recv.at[which], sides[4])

    def rows_done(which):
        return all_of(rows_in.at[which], nb - 1, r_send.at[which], r_recv.at[which], sides[4])

    def gx_done(which):
        return all_of(gx_in.at[which], ngx - 1, s_send.at[which, 0], s_recv.at[which, 0], sides[0])

    def gy_done(which):
        return all_of(gy_in.at[which], ngy - 1, s_send.at[which, 1], s_recv.at[which, 1], sides[2])

    def operand(which):
        return jnp.concatenate(
            [gather[which, pl.ds(x, total_orbs, stride=wx), :] for x in range(wx)], axis=1
        )

    def product(a, b):
        return lax.dot_general(
            a, b, (((1,), (1,)), ((), ())), precision=lax.Precision.HIGHEST, preferred_element_type=F32
        )

    def scatter(which, value):
        blocks = value.reshape(nb, norb, total_orbs)
        rows_out[which, :, 0:norb] = blocks[:, :, 0:128]
        tail[:, 0:norb, 0:32] = blocks[:, :, 128:160]
        for b in range(nb):
            packed = tail[b, 0:8] + pltpu.roll(tail[b, 8:16], 32, 1) + pltpu.roll(tail[b, 16:24], 64, 1)
            rows_out[which, b, 24:32] = packed
        rows_in[which, band] = rows_out[which, band]
        for d in (1, 2, 3, 4, -1, -2, -3):
            peer = lax.rem(band + d + nb, nb)
            pltpu.make_async_remote_copy(
                src_ref=rows_out.at[which, peer],
                dst_ref=rows_in.at[which, band],
                send_sem=r_send.at[which],
                recv_sem=r_recv.at[which],
                device_id={"band": peer},
                device_id_type=MESH,
            ).start()

    def ordered(ref, count):
        value = ref[0]
        for i in range(1, count):
            value = value + ref[i]
        return value

    def over_gx(which):
        rows_done(which).wait_recv()
        gx_in[which, gx] = ordered(rows_in.at[which], nb)
        for d in range(1, ngx):
            pltpu.make_async_remote_copy(
                src_ref=gx_in.at[which, gx],
                dst_ref=gx_in.at[which, gx],
                send_sem=s_send.at[which, 0],
                recv_sem=s_recv.at[which, 0],
                device_id={"gx": lax.rem(gx + d, ngx)},
                device_id_type=MESH,
            ).start()

    def over_gy(which):
        gx_done(which).wait_recv()
        gy_in[which, gy] = ordered(gx_in.at[which], ngx)
        for d in range(1, ngy):
            pltpu.make_async_remote_copy(
                src_ref=gy_in.at[which, gy],
                dst_ref=gy_in.at[which, gy],
                send_sem=s_send.at[which, 1],
                recv_sem=s_recv.at[which, 1],
                device_id={"gy": lax.rem(gy + d, ngy)},
                device_id_type=MESH,
            ).start()

    def finish(which, out):
        gy_done(which).wait_recv()
        value = ordered(gy_in.at[which], ngy) * scale
        out[:, 0:128] = value[0:norb]
        rest = value[24:32]
        out[0:8, 128:160] = rest[:, 0:32]
        out[8:16, 128:160] = pltpu.roll(rest, 96, 1)[:, 0:32]
        out[16:20, 128:160] = pltpu.roll(rest, 64, 1)[0:4, 0:32]

    z_done(0).wait_recv()
    scatter(0, product(operand(0), operand(0)))
    over_gx(0)
    z_done(1).wait_recv()
    one_way = product(operand(0), operand(1))
    scatter(1, one_way + one_way.T)
    over_gy(0)
    over_gx(1)
    finish(0, corr_ref)
    over_gy(1)
    finish(1, proj_ref)

    for level in range(4):
        for side in range(4):
            halo_copy(level, 0, norb, 0, side).wait_send()
    for which in range(2):
        z_done(which).wait_send()
        rows_done(which).wait_send()
        gx_done(which).wait_send()
        gy_done(which).wait_send()
    save.wait()


def body(orbitals, potential):
    norb, wx, wy, nz = orbitals.shape
    ngx, ngy, nb = lax.axis_size("gx"), lax.axis_size("gy"), lax.axis_size("band")
    total = norb * nb
    chunks = norb // PART
    scale = 1.0 / (wx * wy * nz * ngx * ngy)
    block = (norb, wx, wy, nz)
    vmem = pl.BlockSpec(memory_space=pltpu.VMEM)
    hbm = pl.BlockSpec(memory_space=pltpu.HBM)
    return pl.pallas_call(
        functools.partial(kernel, (ngx, ngy, nb), scale),
        out_shape=(
            jax.ShapeDtypeStruct(block, F32),
            jax.ShapeDtypeStruct((norb, total), F32),
            jax.ShapeDtypeStruct((norb, total), F32),
        ),
        in_specs=[hbm, hbm],
        out_specs=(hbm, vmem, vmem),
        scratch_shapes=[
            pltpu.VMEM((5,) + block, F32),
            pltpu.VMEM((4, norb, wx, 24, nz), F32),
            pltpu.VMEM((4,) + block, F32),
            pltpu.VMEM((4,) + block, F32),
            pltpu.VMEM((wx, wy, nz), F32),
            pltpu.VMEM((12, wy, nz), F32),
            pltpu.VMEM((2, chunks, nb, PART * wx, nz), F32),
            pltpu.VMEM((2, total * wx, nz), F32),
            pltpu.VMEM((nb, 24, 128), F32),
            pltpu.VMEM((2, nb, 32, 128), F32),
            pltpu.VMEM((2, nb, 32, 128), F32),
            pltpu.VMEM((2, ngx, 32, 128), F32),
            pltpu.VMEM((2, ngy, 32, 128), F32),
            pltpu.SemaphoreType.DMA((2,)),
            pltpu.SemaphoreType.REGULAR((3,)),
            pltpu.SemaphoreType.DMA((4, 4)),
            pltpu.SemaphoreType.DMA((4, chunks, 4)),
            pltpu.SemaphoreType.DMA((2,)),
            pltpu.SemaphoreType.DMA((2,)),
            pltpu.SemaphoreType.DMA((2,)),
            pltpu.SemaphoreType.DMA((2,)),
            pltpu.SemaphoreType.DMA((2, 2)),
            pltpu.SemaphoreType.DMA((2, 2)),
        ],
        compiler_params=pltpu.CompilerParams(
            collective_id=0, has_side_effects=True, vmem_limit_bytes=48 * 1024 * 1024
        ),
        cost_estimate=pl.CostEstimate(flops=200_000_000, bytes_accessed=2_000_000, transcendentals=0),
    )(orbitals, potential)


def solution(mesh):
    in_specs = (P("band", "gx", "gy", None), P("gx", "gy", None))
    out_specs = (P("band", "gx", "gy", None), P("band", None), P("band", None))
    return jax.shard_map(body, mesh=mesh, in_specs=in_specs, out_specs=out_specs, check_vma=False)
```

```python
import functools

import jax
import jax.numpy as jnp
from jax import lax
from jax.experimental import pallas as pl
from jax.experimental.pallas import tpu as pltpu
from jax.sharding import PartitionSpec as P

stencil_weights = (
    -5369.0 / 1800.0,
    12.0 / 7.0,
    -15.0 / 56.0,
    10.0 / 189.0,
    -1.0 / 112.0,
    2.0 / 1925.0,
    -1.0 / 16632.0,
)
center_level = 7.5
half_width = 4.5

MESH = pl.DeviceIdType.MESH
F32 = jnp.float32
PART = 4


def kernel(
    dims,
    scale,
    v_ref,
    pot_ref,
    filt_ref,
    sums_ref,
    own,
    tall,
    xlo,
    xhi,
    diag,
    shift_w,
    stage,
    gather,
    tail,
    rows_out,
    rows_in,
    gx_in,
    gy_in,
    load_sem,
    ready,
    halo_send,
    halo_recv,
    z_send,
    z_recv,
    r_send,
    r_recv,
    s_send,
    s_recv,
):
    ngx, ngy, nb = dims
    norb, wx, wy, nz = own.shape[1:]
    chunks = norb // PART
    total_orbs = norb * nb
    half_x, half_y = wx // 2, wy // 2
    gx, gy, band = lax.axis_index("gx"), lax.axis_index("gy"), lax.axis_index("band")

    load = pltpu.make_async_copy(v_ref, own.at[0], load_sem.at[0])
    load.start()
    load_pot = pltpu.make_async_copy(pot_ref, diag, load_sem.at[1])
    load_pot.start()

    sides = (
        {"gx": lax.rem(gx + 1, ngx)},
        {"gx": lax.rem(gx + ngx - 1, ngx)},
        {"gy": lax.rem(gy + 1, ngy)},
        {"gy": lax.rem(gy + ngy - 1, ngy)},
        {"band": lax.rem(band + 1, nb)},
        {"band": lax.rem(band + nb - 1, nb)},
    )

    def clear(n, carry):
        for x in range(wx):
            xlo[3, n, x, 0:half_y] = jnp.zeros((half_y, nz), F32)
            xhi[3, n, x, half_y:wy] = jnp.zeros((wy - half_y, nz), F32)
            if x < half_x:
                tall[3, n, x, 0:8] = jnp.zeros((8, nz), F32)
            else:
                tall[3, n, x, 16:24] = jnp.zeros((8, nz), F32)
        return carry

    lax.fori_loop(0, norb, clear, 0)

    barrier = pltpu.get_barrier_semaphore()
    for peer in sides:
        pl.semaphore_signal(barrier, 1, device_id=peer, device_id_type=MESH)

    taps = [0.0] + [-0.5 * w / half_width for w in stencil_weights[1:]]
    lane = lax.broadcasted_iota(jnp.int32, (wy, nz), 1)

    spots = (
        [(0, j) for j in (-2, -1, 1, 2)]
        + [(5, j) for j in (-2, -1, 0, 1)]
        + [(-5, j) for j in (-1, 0, 1, 2)]
    )
    for i, (far, j) in enumerate(spots):
        where = lane + far
        where = jnp.where(where >= nz, where - nz, jnp.where(where < 0, where + nz, where))
        source = where - (far + j)
        inside = jnp.logical_and(source >= 0, source < nz)
        shift_w[i] = jnp.where(inside, taps[abs(far + j)], 0.0)

    tail[...] = jnp.zeros_like(tail)
    load.wait()
    load_pot.wait()
    diag[...] = (diag[...] - 1.5 * stencil_weights[0] - center_level) * (1.0 / half_width)

    def fill(n, carry):
        for x in range(wx):
            tall[0, n, x, 8:16] = own[0, n, x]
        return carry

    lax.fori_loop(0, norb, fill, 0)
    pl.semaphore_wait(barrier, 6)

    def relay(turn):
        for peer in sides:
            pl.semaphore_signal(ready.at[turn], 1, device_id=peer, device_id_type=MESH)

    def heard(turn):
        pl.semaphore_wait(ready.at[turn], 6)

    def halo_copy(level, start, count, sem_at, side):
        group = pl.ds(start, count)
        if level < 3:
            src = (
                own.at[level, group],
                own.at[level, group],
                own.at[level, group, :, 2:8],
                own.at[level, group, :, 0:6],
            )[side]
            dst = (
                xlo.at[level, group],
                xhi.at[level, group],
                tall.at[level, group, :, 2:8],
                tall.at[level, group, :, 16:22],
            )[side]
        else:
            src = (
                own.at[level, group, :, half_y:wy],
                own.at[level, group, :, 0:half_y],
                own.at[level, group, half_x:wx, 2:8],
                own.at[level, group, 0:half_x, 0:6],
            )[side]
            dst = (
                xlo.at[level, group, :, half_y:wy],
                xhi.at[level, group, :, 0:half_y],
                tall.at[level, group, half_x:wx, 2:8],
                tall.at[level, group, 0:half_x, 16:22],
            )[side]
        return pltpu.make_async_remote_copy(
            src_ref=src,
            dst_ref=dst,
            send_sem=halo_send.at[level, side],
            recv_sem=halo_recv.at[level, sem_at, side],
            device_id=sides[side],
            device_id_type=MESH,
        )

    def halo_start(level, c):
        for side in (2, 3, 0, 1):
            halo_copy(level, c * PART, PART, c, side).start()

    def halo_wait(level, c):
        for side in (0, 1, 2, 3):
            halo_copy(level, c * PART, PART, c, side).wait_recv()

    def base(level, n):
        inner = [own[level, n, x] for x in range(wx)]
        if level == 3:
            inner = [0.5 * v for v in inner]
        line = [xlo[level, n, x] for x in range(wx)] + inner + [xhi[level, n, x] for x in range(wx)]
        out = []
        for x in range(wx):
            v = inner[x]
            total = diag[x] * v
            for k in range(1, 7):
                near = line[wx + x + k] + line[wx + x - k]
                near += tall[level, n, x, 8 + k : 16 + k] + tall[level, n, x, 8 - k : 16 - k]
                total += taps[k] * near
            rolled = {0: v}
            for j in (-2, -1, 1, 2):
                rolled[j] = pltpu.roll(v, j % nz, 1)
            parts = {0: None, 5: None, -5: None}
            for i, (far, j) in enumerate(spots):
                term = shift_w[i] * rolled[j]
                parts[far] = term if parts[far] is None else parts[far] + term
            total += parts[0]
            total += pltpu.roll(parts[5], 5, 1) + pltpu.roll(parts[-5], nz - 5, 1)
            out.append(total)
        return out

    def z_rows(c):
        return pl.ds(pl.multiple_of(band * (norb * wx) + c * (PART * wx), 8), PART * wx)

    def spread(which, c, value):
        stage[which, c] = jnp.swapaxes(value, 0, 1)
        gather[which, z_rows(c)] = stage[which, c, band]
        for d in (1, 2, 3, 4, -1, -2, -3):
            peer = lax.rem(band + d + nb, nb)
            pltpu.make_async_remote_copy(
                src_ref=stage.at[which, c, peer],
                dst_ref=gather.at[which, z_rows(c)],
                send_sem=z_send.at[which],
                recv_sem=z_recv.at[which],
                device_id={"band": peer},
                device_id_type=MESH,
            ).start()

    def step(level, c):
        halo_wait(level, c)

        def one(i, carry):
            n = c * PART + i
            for x, value in enumerate(base(level, n)):
                if level in (1, 2):
                    value = 2.0 * value - own[level - 1, n, x]
                elif level == 3:
                    value = half_width * value + (0.5 * center_level) * own[3, n, x]
                own[level + 1, n, x] = value
                if level < 3:
                    tall[level + 1, n, x, 8:16] = 0.5 * value if level == 2 else value
            return carry

        lax.fori_loop(0, PART, one, 0, unroll=4)
        if level < 3:
            halo_start(level + 1, c)
        if level >= 2:
            spread(level - 2, c, own[level + 1, pl.ds(c * PART, PART)].reshape(PART * wx, wy, nz))

    def run(level, first, end):
        def body(c, carry):
            if level < 0:
                halo_start(0, c)
            else:
                step(level, c)
            return carry

        lax.fori_loop(first, end, body, 0)

    cut = (chunks + 1) // 2
    run(-1, 0, cut)
    relay(0)
    heard(0)
    relay(1)
    run(0, 0, cut)
    heard(1)
    relay(2)
    run(1, 0, cut)
    run(-1, cut, chunks)
    heard(2)
    run(2, 0, cut)
    run(0, cut, chunks)
    run(3, 0, cut)
    run(1, cut, chunks)
    run(2, cut, chunks)
    save = pltpu.make_async_copy(own.at[3], filt_ref, load_sem.at[0])
    save.start()
    run(3, cut, chunks)

    def all_of(ref, count, send, recv, peer):
        part = ref.at[pl.ds(0, count)]
        return pltpu.make_async_remote_copy(
            src_ref=part, dst_ref=part, send_sem=send, recv_sem=recv, device_id=peer, device_id_type=MESH
        )

    def z_done(which):
        return all_of(gather.at[which], norb * wx * (nb - 1), z_send.at[which], z_recv.at[which], sides[4])

    def rows_done(which):
        return all_of(rows_in.at[which], nb - 1, r_send.at[which], r_recv.at[which], sides[4])

    def gx_done(which):
        return all_of(gx_in.at[which], ngx - 1, s_send.at[which, 0], s_recv.at[which, 0], sides[0])

    def gy_done(which):
        return all_of(gy_in.at[which], ngy - 1, s_send.at[which, 1], s_recv.at[which, 1], sides[2])

    def operand(which):
        return jnp.concatenate(
            [gather[which, pl.ds(x, total_orbs, stride=wx), :] for x in range(wx)], axis=1
        )

    def product(a, b):
        return lax.dot_general(
            a, b, (((1,), (1,)), ((), ())), precision=lax.Precision.HIGHEST, preferred_element_type=F32
        )

    def scatter(which, value):
        blocks = value.reshape(nb, norb, total_orbs)
        rows_out[which, :, 0:norb] = blocks[:, :, 0:128]
        tail[:, 0:norb, 0:32] = blocks[:, :, 128:160]
        for b in range(nb):
            packed = tail[b, 0:8] + pltpu.roll(tail[b, 8:16], 32, 1) + pltpu.roll(tail[b, 16:24], 64, 1)
            rows_out[which, b, 24:32] = packed
        rows_in[which, band] = rows_out[which, band]
        for d in (1, 2, 3, 4, -1, -2, -3):
            peer = lax.rem(band + d + nb, nb)
            pltpu.make_async_remote_copy(
                src_ref=rows_out.at[which, peer],
                dst_ref=rows_in.at[which, band],
                send_sem=r_send.at[which],
                recv_sem=r_recv.at[which],
                device_id={"band": peer},
                device_id_type=MESH,
            ).start()

    def ordered(ref, count):
        value = ref[0]
        for i in range(1, count):
            value = value + ref[i]
        return value

    def over_gx(which):
        rows_done(which).wait_recv()
        gx_in[which, gx] = ordered(rows_in.at[which], nb)
        for d in range(1, ngx):
            pltpu.make_async_remote_copy(
                src_ref=gx_in.at[which, gx],
                dst_ref=gx_in.at[which, gx],
                send_sem=s_send.at[which, 0],
                recv_sem=s_recv.at[which, 0],
                device_id={"gx": lax.rem(gx + d, ngx)},
                device_id_type=MESH,
            ).start()

    def over_gy(which):
        gx_done(which).wait_recv()
        gy_in[which, gy] = ordered(gx_in.at[which], ngx)
        for d in range(1, ngy):
            pltpu.make_async_remote_copy(
                src_ref=gy_in.at[which, gy],
                dst_ref=gy_in.at[which, gy],
                send_sem=s_send.at[which, 1],
                recv_sem=s_recv.at[which, 1],
                device_id={"gy": lax.rem(gy + d, ngy)},
                device_id_type=MESH,
            ).start()

    def finish(which):
        gy_done(which).wait_recv()
        sums_ref[which] = ordered(gy_in.at[which], ngy) * scale

    z_done(0).wait_recv()
    scatter(0, product(operand(0), operand(0)))
    z_done(1).wait_recv()
    one_way = product(operand(0), operand(1))
    scatter(1, one_way + one_way.T)
    over_gx(0)
    over_gy(0)
    over_gx(1)
    finish(0)
    over_gy(1)
    finish(1)

    for level in range(4):
        for side in range(4):
            halo_copy(level, 0, norb, 0, side).wait_send()
    for which in range(2):
        z_done(which).wait_send()
        rows_done(which).wait_send()
        gx_done(which).wait_send()
        gy_done(which).wait_send()
    save.wait()


def deliver(sums_ref, filt_ref, out_ref, corr_ref, proj_ref):
    out_ref[...] = filt_ref[...]
    norb = corr_ref.shape[0]
    for which, out in enumerate((corr_ref, proj_ref)):
        value = sums_ref[which]
        out[:, 0:128] = value[0:norb]
        rest = value[24:32]
        out[0:8, 128:160] = rest[:, 0:32]
        out[8:16, 128:160] = pltpu.roll(rest, 96, 1)[:, 0:32]
        out[16:20, 128:160] = pltpu.roll(rest, 64, 1)[0:4, 0:32]


def body(orbitals, potential):
    norb, wx, wy, nz = orbitals.shape
    ngx, ngy, nb = lax.axis_size("gx"), lax.axis_size("gy"), lax.axis_size("band")
    total = norb * nb
    chunks = norb // PART
    scale = 1.0 / (wx * wy * nz * ngx * ngy)
    block = (norb, wx, wy, nz)
    vmem = pl.BlockSpec(memory_space=pltpu.VMEM)
    hbm = pl.BlockSpec(memory_space=pltpu.HBM)
    filtered, sums = pl.pallas_call(
        functools.partial(kernel, (ngx, ngy, nb), scale),
        out_shape=(
            jax.ShapeDtypeStruct(block, F32),
            jax.ShapeDtypeStruct((2, 32, 128), F32),
        ),
        in_specs=[hbm, hbm],
        out_specs=(hbm, vmem),
        scratch_shapes=[
            pltpu.VMEM((5,) + block, F32),
            pltpu.VMEM((4, norb, wx, 24, nz), F32),
            pltpu.VMEM((4,) + block, F32),
            pltpu.VMEM((4,) + block, F32),
            pltpu.VMEM((wx, wy, nz), F32),
            pltpu.VMEM((12, wy, nz), F32),
            pltpu.VMEM((2, chunks, nb, PART * wx, nz), F32),
            pltpu.VMEM((2, total * wx, nz), F32),
            pltpu.VMEM((nb, 24, 128), F32),
            pltpu.VMEM((2, nb, 32, 128), F32),
            pltpu.VMEM((2, nb, 32, 128), F32),
            pltpu.VMEM((2, ngx, 32, 128), F32),
            pltpu.VMEM((2, ngy, 32, 128), F32),
            pltpu.SemaphoreType.DMA((2,)),
            pltpu.SemaphoreType.REGULAR((3,)),
            pltpu.SemaphoreType.DMA((4, 4)),
            pltpu.SemaphoreType.DMA((4, chunks, 4)),
            pltpu.SemaphoreType.DMA((2,)),
            pltpu.SemaphoreType.DMA((2,)),
            pltpu.SemaphoreType.DMA((2,)),
            pltpu.SemaphoreType.DMA((2,)),
            pltpu.SemaphoreType.DMA((2, 2)),
            pltpu.SemaphoreType.DMA((2, 2)),
        ],
        compiler_params=pltpu.CompilerParams(
            collective_id=0, has_side_effects=True, vmem_limit_bytes=60 * 1024 * 1024
        ),
        cost_estimate=pl.CostEstimate(flops=200_000_000, bytes_accessed=2_000_000, transcendentals=0),
    )(orbitals, potential)
    return pl.pallas_call(
        deliver,
        out_shape=(
            jax.ShapeDtypeStruct(block, F32),
            jax.ShapeDtypeStruct((norb, total), F32),
            jax.ShapeDtypeStruct((norb, total), F32),
        ),
        in_specs=[vmem, vmem],
        out_specs=(vmem, vmem, vmem),
        cost_estimate=pl.CostEstimate(flops=10_000, bytes_accessed=1_000_000, transcendentals=0),
    )(sums, filtered)


def solution(mesh):
    in_specs = (P("band", "gx", "gy", None), P("gx", "gy", None))
    out_specs = (P("band", "gx", "gy", None), P("band", None), P("band", None))
    return jax.shard_map(body, mesh=mesh, in_specs=in_specs, out_specs=out_specs, check_vma=False)
```

```python
import functools

import jax
import jax.numpy as jnp
from jax import lax
from jax.experimental import pallas as pl
from jax.experimental.pallas import tpu as pltpu
from jax.sharding import PartitionSpec as P

stencil_weights = (
    -5369.0 / 1800.0,
    12.0 / 7.0,
    -15.0 / 56.0,
    10.0 / 189.0,
    -1.0 / 112.0,
    2.0 / 1925.0,
    -1.0 / 16632.0,
)
center_level = 7.5
half_width = 4.5

MESH = pl.DeviceIdType.MESH
F32 = jnp.float32
PART = 4


def kernel(
    dims,
    scale,
    v_ref,
    pot_ref,
    filt_ref,
    sums_ref,
    own,
    tall,
    xlo,
    xhi,
    diag,
    shift_w,
    stage,
    gather,
    tail,
    rows_out,
    rows_in,
    gx_in,
    gy_in,
    load_sem,
    ready,
    halo_send,
    halo_recv,
    z_send,
    z_recv,
    r_send,
    r_recv,
    s_send,
    s_recv,
):
    ngx, ngy, nb = dims
    norb, wx, wy, nz = own.shape[1:]
    chunks = norb // PART
    total_orbs = norb * nb
    half_x, half_y = wx // 2, wy // 2
    gx, gy, band = lax.axis_index("gx"), lax.axis_index("gy"), lax.axis_index("band")

    load = pltpu.make_async_copy(v_ref, own.at[0], load_sem.at[0])
    load.start()
    load_pot = pltpu.make_async_copy(pot_ref, diag, load_sem.at[1])
    load_pot.start()

    sides = (
        {"gx": lax.rem(gx + 1, ngx)},
        {"gx": lax.rem(gx + ngx - 1, ngx)},
        {"gy": lax.rem(gy + 1, ngy)},
        {"gy": lax.rem(gy + ngy - 1, ngy)},
        {"band": lax.rem(band + 1, nb)},
        {"band": lax.rem(band + nb - 1, nb)},
    )

    barrier = pltpu.get_barrier_semaphore()
    for peer in sides:
        pl.semaphore_signal(barrier, 1, device_id=peer, device_id_type=MESH)

    def clear(n, carry):
        for x in range(wx):
            xlo[3, n, x, 0:half_y] = jnp.zeros((half_y, nz), F32)
            xhi[3, n, x, half_y:wy] = jnp.zeros((wy - half_y, nz), F32)
            if x < half_x:
                tall[3, n, x, 0:8] = jnp.zeros((8, nz), F32)
            else:
                tall[3, n, x, 16:24] = jnp.zeros((8, nz), F32)
        return carry

    lax.fori_loop(0, norb, clear, 0)

    taps = [0.0] + [-0.5 * w / half_width for w in stencil_weights[1:]]
    lane = lax.broadcasted_iota(jnp.int32, (wy, nz), 1)

    spots = (
        [(0, j) for j in (-2, -1, 1, 2)]
        + [(5, j) for j in (-2, -1, 0, 1)]
        + [(-5, j) for j in (-1, 0, 1, 2)]
    )
    for i, (far, j) in enumerate(spots):
        where = lane + far
        where = jnp.where(where >= nz, where - nz, jnp.where(where < 0, where + nz, where))
        source = where - (far + j)
        inside = jnp.logical_and(source >= 0, source < nz)
        shift_w[i] = jnp.where(inside, taps[abs(far + j)], 0.0)

    tail[...] = jnp.zeros_like(tail)
    load.wait()
    pl.semaphore_wait(barrier, 6)

    def relay(turn):
        for peer in sides[4:]:
            pl.semaphore_signal(ready.at[turn], 1, device_id=peer, device_id_type=MESH)

    def heard(turn):
        pl.semaphore_wait(ready.at[turn], 2)

    def halo_copy(level, start, count, sem_at, side):
        group = pl.ds(start, count)
        if level < 3:
            src = (
                own.at[level, group],
                own.at[level, group],
                own.at[level, group, :, 2:8],
                own.at[level, group, :, 0:6],
            )[side]
            dst = (
                xlo.at[level, group],
                xhi.at[level, group],
                tall.at[level, group, :, 2:8],
                tall.at[level, group, :, 16:22],
            )[side]
        else:
            src = (
                own.at[level, group, :, half_y:wy],
                own.at[level, group, :, 0:half_y],
                own.at[level, group, half_x:wx, 2:8],
                own.at[level, group, 0:half_x, 0:6],
            )[side]
            dst = (
                xlo.at[level, group, :, half_y:wy],
                xhi.at[level, group, :, 0:half_y],
                tall.at[level, group, half_x:wx, 2:8],
                tall.at[level, group, 0:half_x, 16:22],
            )[side]
        return pltpu.make_async_remote_copy(
            src_ref=src,
            dst_ref=dst,
            send_sem=halo_send.at[level, side],
            recv_sem=halo_recv.at[level, sem_at, side],
            device_id=sides[side],
            device_id_type=MESH,
        )

    def halo_start(level, c):
        for side in (2, 3, 0, 1):
            halo_copy(level, c * PART, PART, c, side).start()

    def halo_wait(level, c):
        for side in (0, 1, 2, 3):
            halo_copy(level, c * PART, PART, c, side).wait_recv()

    def base(level, n):
        inner = [own[level, n, x] for x in range(wx)]
        if level == 3:
            inner = [0.5 * v for v in inner]
        line = [xlo[level, n, x] for x in range(wx)] + inner + [xhi[level, n, x] for x in range(wx)]
        out = []
        for x in range(wx):
            v = inner[x]
            total = diag[x] * v
            for k in range(1, 7):
                near = line[wx + x + k] + line[wx + x - k]
                near += tall[level, n, x, 8 + k : 16 + k] + tall[level, n, x, 8 - k : 16 - k]
                total += taps[k] * near
            rolled = {0: v}
            for j in (-2, -1, 1, 2):
                rolled[j] = pltpu.roll(v, j % nz, 1)
            parts = {0: None, 5: None, -5: None}
            for i, (far, j) in enumerate(spots):
                term = shift_w[i] * rolled[j]
                parts[far] = term if parts[far] is None else parts[far] + term
            total += parts[0]
            total += pltpu.roll(parts[5], 5, 1) + pltpu.roll(parts[-5], nz - 5, 1)
            out.append(total)
        return out

    def z_rows(c):
        return pl.ds(pl.multiple_of(band * (norb * wx) + c * (PART * wx), 8), PART * wx)

    def spread(which, c, value):
        stage[which, c] = jnp.swapaxes(value, 0, 1)
        gather[which, z_rows(c)] = stage[which, c, band]
        for d in (4, 3, -3, 2, -2, 1, -1):
            peer = lax.rem(band + d + nb, nb)
            pltpu.make_async_remote_copy(
                src_ref=stage.at[which, c, peer],
                dst_ref=gather.at[which, z_rows(c)],
                send_sem=z_send.at[which],
                recv_sem=z_recv.at[which],
                device_id={"band": peer},
                device_id_type=MESH,
            ).start()

    def step(level, c):
        halo_wait(level, c)

        def one(i, carry):
            n = c * PART + i
            for x, value in enumerate(base(level, n)):
                if level in (1, 2):
                    value = 2.0 * value - own[level - 1, n, x]
                elif level == 3:
                    value = half_width * value + (0.5 * center_level) * own[3, n, x]
                own[level + 1, n, x] = value
                if level < 3:
                    tall[level + 1, n, x, 8:16] = 0.5 * value if level == 2 else value
            return carry

        lax.fori_loop(0, PART, one, 0, unroll=4)
        if level < 3:
            halo_start(level + 1, c)
        if level >= 2:
            spread(level - 2, c, own[level + 1, pl.ds(c * PART, PART)].reshape(PART * wx, wy, nz))

    def run(level, first, end):
        def body(c, carry):
            if level < 0:
                halo_start(0, c)
            else:
                step(level, c)
            return carry

        lax.fori_loop(first, end, body, 0)

    cut = (chunks + 1) // 2
    run(-1, 0, cut)
    relay(0)
    load_pot.wait()
    diag[...] = (diag[...] - 1.5 * stencil_weights[0] - center_level) * (1.0 / half_width)

    def fill(n, carry):
        for x in range(wx):
            tall[0, n, x, 8:16] = own[0, n, x]
        return carry

    lax.fori_loop(0, norb, fill, 0)
    heard(0)
    relay(1)
    run(0, 0, cut)
    heard(1)
    relay(2)
    run(1, 0, cut)
    run(-1, cut, chunks)
    heard(2)
    run(2, 0, cut)
    run(0, cut, chunks)
    run(3, 0, cut)
    run(1, cut, chunks)
    run(2, cut, chunks)
    save = pltpu.make_async_copy(own.at[3], filt_ref, load_sem.at[0])
    save.start()
    run(3, cut, chunks)

    def all_of(ref, count, send, recv, peer):
        part = ref.at[pl.ds(0, count)]
        return pltpu.make_async_remote_copy(
            src_ref=part, dst_ref=part, send_sem=send, recv_sem=recv, device_id=peer, device_id_type=MESH
        )

    def z_done(which):
        return all_of(gather.at[which], norb * wx * (nb - 1), z_send.at[which], z_recv.at[which], sides[4])

    def rows_done(which):
        return all_of(rows_in.at[which], nb - 1, r_send.at[which], r_recv.at[which], sides[4])

    def gx_done(which):
        return all_of(gx_in.at[which], ngx - 1, s_send.at[which, 0], s_recv.at[which, 0], sides[0])

    def gy_done(which):
        return all_of(gy_in.at[which], ngy - 1, s_send.at[which, 1], s_recv.at[which, 1], sides[2])

    def operand(which):
        return jnp.concatenate(
            [gather[which, pl.ds(x, total_orbs, stride=wx), :] for x in range(wx)], axis=1
        )

    def product(a, b):
        return lax.dot_general(
            a, b, (((1,), (1,)), ((), ())), precision=lax.Precision.HIGHEST, preferred_element_type=F32
        )

    def scatter(which, value):
        blocks = value.reshape(nb, norb, total_orbs)
        rows_out[which, :, 0:norb] = blocks[:, :, 0:128]
        tail[:, 0:norb, 0:32] = blocks[:, :, 128:160]
        for b in range(nb):
            packed = tail[b, 0:8] + pltpu.roll(tail[b, 8:16], 32, 1) + pltpu.roll(tail[b, 16:24], 64, 1)
            rows_out[which, b, 24:32] = packed
        rows_in[which, band] = rows_out[which, band]
        for d in (4, 3, -3, 2, -2, 1, -1):
            peer = lax.rem(band + d + nb, nb)
            pltpu.make_async_remote_copy(
                src_ref=rows_out.at[which, peer],
                dst_ref=rows_in.at[which, band],
                send_sem=r_send.at[which],
                recv_sem=r_recv.at[which],
                device_id={"band": peer},
                device_id_type=MESH,
            ).start()

    def ordered(ref, count):
        value = ref[0]
        for i in range(1, count):
            value = value + ref[i]
        return value

    def over_gx(which):
        rows_done(which).wait_recv()
        gx_in[which, gx] = ordered(rows_in.at[which], nb)
        for d in (4, 3, 5, 2, 6, 1, 7):
            pltpu.make_async_remote_copy(
                src_ref=gx_in.at[which, gx],
                dst_ref=gx_in.at[which, gx],
                send_sem=s_send.at[which, 0],
                recv_sem=s_recv.at[which, 0],
                device_id={"gx": lax.rem(gx + d, ngx)},
                device_id_type=MESH,
            ).start()

    def over_gy(which):
        gx_done(which).wait_recv()
        gy_in[which, gy] = ordered(gx_in.at[which], ngx)
        for d in (2, 1, 3):
            pltpu.make_async_remote_copy(
                src_ref=gy_in.at[which, gy],
                dst_ref=gy_in.at[which, gy],
                send_sem=s_send.at[which, 1],
                recv_sem=s_recv.at[which, 1],
                device_id={"gy": lax.rem(gy + d, ngy)},
                device_id_type=MESH,
            ).start()

    def finish(which):
        gy_done(which).wait_recv()
        sums_ref[which] = ordered(gy_in.at[which], ngy) * scale

    z_done(0).wait_recv()
    scatter(0, product(operand(0), operand(0)))
    z_done(1).wait_recv()
    one_way = product(operand(0), operand(1))
    scatter(1, one_way + one_way.T)
    over_gx(0)
    over_gy(0)
    over_gx(1)
    finish(0)
    over_gy(1)
    finish(1)

    for level in range(4):
        for side in range(4):
            halo_copy(level, 0, norb, 0, side).wait_send()
    for which in range(2):
        z_done(which).wait_send()
        rows_done(which).wait_send()
        gx_done(which).wait_send()
        gy_done(which).wait_send()
    save.wait()


def deliver(sums_ref, filt_ref, out_ref, corr_ref, proj_ref):
    out_ref[...] = filt_ref[...]
    norb = corr_ref.shape[0]
    for which, out in enumerate((corr_ref, proj_ref)):
        value = sums_ref[which]
        out[:, 0:128] = value[0:norb]
        rest = value[24:32]
        out[0:8, 128:160] = rest[:, 0:32]
        out[8:16, 128:160] = pltpu.roll(rest, 96, 1)[:, 0:32]
        out[16:20, 128:160] = pltpu.roll(rest, 64, 1)[0:4, 0:32]


def body(orbitals, potential):
    norb, wx, wy, nz = orbitals.shape
    ngx, ngy, nb = lax.axis_size("gx"), lax.axis_size("gy"), lax.axis_size("band")
    total = norb * nb
    chunks = norb // PART
    scale = 1.0 / (wx * wy * nz * ngx * ngy)
    block = (norb, wx, wy, nz)
    vmem = pl.BlockSpec(memory_space=pltpu.VMEM)
    hbm = pl.BlockSpec(memory_space=pltpu.HBM)
    filtered, sums = pl.pallas_call(
        functools.partial(kernel, (ngx, ngy, nb), scale),
        out_shape=(
            jax.ShapeDtypeStruct(block, F32),
            jax.ShapeDtypeStruct((2, 32, 128), F32),
        ),
        in_specs=[hbm, hbm],
        out_specs=(hbm, vmem),
        scratch_shapes=[
            pltpu.VMEM((5,) + block, F32),
            pltpu.VMEM((4, norb, wx, 24, nz), F32),
            pltpu.VMEM((4,) + block, F32),
            pltpu.VMEM((4,) + block, F32),
            pltpu.VMEM((wx, wy, nz), F32),
            pltpu.VMEM((12, wy, nz), F32),
            pltpu.VMEM((2, chunks, nb, PART * wx, nz), F32),
            pltpu.VMEM((2, total * wx, nz), F32),
            pltpu.VMEM((nb, 24, 128), F32),
            pltpu.VMEM((2, nb, 32, 128), F32),
            pltpu.VMEM((2, nb, 32, 128), F32),
            pltpu.VMEM((2, ngx, 32, 128), F32),
            pltpu.VMEM((2, ngy, 32, 128), F32),
            pltpu.SemaphoreType.DMA((2,)),
            pltpu.SemaphoreType.REGULAR((3,)),
            pltpu.SemaphoreType.DMA((4, 4)),
            pltpu.SemaphoreType.DMA((4, chunks, 4)),
            pltpu.SemaphoreType.DMA((2,)),
            pltpu.SemaphoreType.DMA((2,)),
            pltpu.SemaphoreType.DMA((2,)),
            pltpu.SemaphoreType.DMA((2,)),
            pltpu.SemaphoreType.DMA((2, 2)),
            pltpu.SemaphoreType.DMA((2, 2)),
        ],
        compiler_params=pltpu.CompilerParams(
            collective_id=0, has_side_effects=True, vmem_limit_bytes=60 * 1024 * 1024
        ),
        cost_estimate=pl.CostEstimate(flops=200_000_000, bytes_accessed=2_000_000, transcendentals=0),
    )(orbitals, potential)
    return pl.pallas_call(
        deliver,
        out_shape=(
            jax.ShapeDtypeStruct(block, F32),
            jax.ShapeDtypeStruct((norb, total), F32),
            jax.ShapeDtypeStruct((norb, total), F32),
        ),
        in_specs=[vmem, vmem],
        out_specs=(vmem, vmem, vmem),
        cost_estimate=pl.CostEstimate(flops=10_000, bytes_accessed=1_000_000, transcendentals=0),
    )(sums, filtered)


def solution(mesh):
    in_specs = (P("band", "gx", "gy", None), P("gx", "gy", None))
    out_specs = (P("band", "gx", "gy", None), P("band", None), P("band", None))
    return jax.shard_map(body, mesh=mesh, in_specs=in_specs, out_specs=out_specs, check_vma=False)
```

```python
import functools

import jax
import jax.numpy as jnp
from jax import lax
from jax.experimental import pallas as pl
from jax.experimental.pallas import tpu as pltpu
from jax.sharding import PartitionSpec as P

stencil_weights = (
    -5369.0 / 1800.0,
    12.0 / 7.0,
    -15.0 / 56.0,
    10.0 / 189.0,
    -1.0 / 112.0,
    2.0 / 1925.0,
    -1.0 / 16632.0,
)
center_level = 7.5
half_width = 4.5

MESH = pl.DeviceIdType.MESH
F32 = jnp.float32
PART = 4


def kernel(
    dims,
    scale,
    v_ref,
    pot_ref,
    filt_ref,
    sums_ref,
    own,
    tall,
    xlo,
    xhi,
    diag,
    shift_w,
    stage,
    gather,
    tail,
    rows_out,
    rows_in,
    gx_in,
    gy_in,
    load_sem,
    ready,
    halo_send,
    halo_recv,
    z_send,
    z_recv,
    r_send,
    r_recv,
    s_send,
    s_recv,
):
    ngx, ngy, nb = dims
    norb, wx, wy, nz = own.shape[1:]
    chunks = norb // PART
    total_orbs = norb * nb
    half_x, half_y = wx // 2, wy // 2
    gx, gy, band = lax.axis_index("gx"), lax.axis_index("gy"), lax.axis_index("band")

    load = pltpu.make_async_copy(v_ref, own.at[0], load_sem.at[0])
    load.start()
    load_pot = pltpu.make_async_copy(pot_ref, diag, load_sem.at[1])
    load_pot.start()

    sides = (
        {"gx": lax.rem(gx + 1, ngx)},
        {"gx": lax.rem(gx + ngx - 1, ngx)},
        {"gy": lax.rem(gy + 1, ngy)},
        {"gy": lax.rem(gy + ngy - 1, ngy)},
        {"band": lax.rem(band + 1, nb)},
        {"band": lax.rem(band + nb - 1, nb)},
    )

    barrier = pltpu.get_barrier_semaphore()
    for peer in sides:
        pl.semaphore_signal(barrier, 1, device_id=peer, device_id_type=MESH)

    def clear(n, carry):
        for x in range(wx):
            xlo[3, n, x, 0:half_y] = jnp.zeros((half_y, nz), F32)
            xhi[3, n, x, half_y:wy] = jnp.zeros((wy - half_y, nz), F32)
            if x < half_x:
                tall[3, n, x, 0:8] = jnp.zeros((8, nz), F32)
            else:
                tall[3, n, x, 16:24] = jnp.zeros((8, nz), F32)
        return carry

    lax.fori_loop(0, norb, clear, 0)

    taps = [0.0] + [-0.5 * w / half_width for w in stencil_weights[1:]]
    lane = lax.broadcasted_iota(jnp.int32, (wy, nz), 1)

    spots = (
        [(0, j) for j in (-2, -1, 1, 2)]
        + [(5, j) for j in (-2, -1, 0, 1)]
        + [(-5, j) for j in (-1, 0, 1, 2)]
    )
    for i, (far, j) in enumerate(spots):
        where = lane + far
        where = jnp.where(where >= nz, where - nz, jnp.where(where < 0, where + nz, where))
        source = where - (far + j)
        inside = jnp.logical_and(source >= 0, source < nz)
        shift_w[i] = jnp.where(inside, taps[abs(far + j)], 0.0)

    tail[...] = jnp.zeros_like(tail)
    load.wait()
    pl.semaphore_wait(barrier, 6)

    def relay(turn):
        for peer in sides[4:]:
            pl.semaphore_signal(ready.at[turn], 1, device_id=peer, device_id_type=MESH)

    def heard(turn):
        pl.semaphore_wait(ready.at[turn], 2)

    def halo_copy(level, start, count, sem_at, side):
        group = pl.ds(start, count)
        if level < 3:
            src = (
                own.at[level, group],
                own.at[level, group],
                own.at[level, group, :, 2:8],
                own.at[level, group, :, 0:6],
            )[side]
            dst = (
                xlo.at[level, group],
                xhi.at[level, group],
                tall.at[level, group, :, 2:8],
                tall.at[level, group, :, 16:22],
            )[side]
        else:
            src = (
                own.at[level, group, :, half_y:wy],
                own.at[level, group, :, 0:half_y],
                own.at[level, group, half_x:wx, 2:8],
                own.at[level, group, 0:half_x, 0:6],
            )[side]
            dst = (
                xlo.at[level, group, :, half_y:wy],
                xhi.at[level, group, :, 0:half_y],
                tall.at[level, group, half_x:wx, 2:8],
                tall.at[level, group, 0:half_x, 16:22],
            )[side]
        return pltpu.make_async_remote_copy(
            src_ref=src,
            dst_ref=dst,
            send_sem=halo_send.at[level, side],
            recv_sem=halo_recv.at[level, sem_at, side],
            device_id=sides[side],
            device_id_type=MESH,
        )

    def halo_start(level, c):
        for side in (2, 3, 0, 1):
            halo_copy(level, c * PART, PART, c, side).start()

    def halo_wait(level, c):
        for side in (0, 1, 2, 3):
            halo_copy(level, c * PART, PART, c, side).wait_recv()

    def base(level, n):
        inner = [own[level, n, x] for x in range(wx)]
        if level == 3:
            inner = [0.5 * v for v in inner]
        line = [xlo[level, n, x] for x in range(wx)] + inner + [xhi[level, n, x] for x in range(wx)]
        out = []
        for x in range(wx):
            v = inner[x]
            total = diag[x] * v
            for k in range(1, 7):
                near = line[wx + x + k] + line[wx + x - k]
                near += tall[level, n, x, 8 + k : 16 + k] + tall[level, n, x, 8 - k : 16 - k]
                total += taps[k] * near
            rolled = {0: v}
            for j in (-2, -1, 1, 2):
                rolled[j] = pltpu.roll(v, j % nz, 1)
            parts = {0: None, 5: None, -5: None}
            for i, (far, j) in enumerate(spots):
                term = shift_w[i] * rolled[j]
                parts[far] = term if parts[far] is None else parts[far] + term
            total += parts[0]
            total += pltpu.roll(parts[5], 5, 1) + pltpu.roll(parts[-5], nz - 5, 1)
            out.append(total)
        return out

    def z_rows(c):
        return pl.ds(pl.multiple_of(band * (norb * wx) + c * (PART * wx), 8), PART * wx)

    def spread(which, c, value):
        stage[which, c] = jnp.swapaxes(value, 0, 1)
        gather[which, z_rows(c)] = stage[which, c, band]
        for d in (4, 3, -3, 2, -2, 1, -1):
            peer = lax.rem(band + d + nb, nb)
            pltpu.make_async_remote_copy(
                src_ref=stage.at[which, c, peer],
                dst_ref=gather.at[which, z_rows(c)],
                send_sem=z_send.at[which],
                recv_sem=z_recv.at[which],
                device_id={"band": peer},
                device_id_type=MESH,
            ).start()

    def step(level, c):
        halo_wait(level, c)

        def one(i, carry):
            n = c * PART + i
            for x, value in enumerate(base(level, n)):
                if level in (1, 2):
                    value = 2.0 * value - own[level - 1, n, x]
                elif level == 3:
                    value = half_width * value + (0.5 * center_level) * own[3, n, x]
                own[level + 1, n, x] = value
                if level < 3:
                    tall[level + 1, n, x, 8:16] = 0.5 * value if level == 2 else value
            return carry

        lax.fori_loop(0, PART, one, 0, unroll=4)
        if level < 3:
            halo_start(level + 1, c)
        if level >= 2:
            spread(level - 2, c, own[level + 1, pl.ds(c * PART, PART)].reshape(PART * wx, wy, nz))

    def run(level, first, end):
        def body(c, carry):
            if level < 0:
                halo_start(0, c)
            else:
                step(level, c)
            return carry

        lax.fori_loop(first, end, body, 0)

    cut = (chunks + 1) // 2
    run(-1, 0, cut)
    relay(0)
    load_pot.wait()
    diag[...] = (diag[...] - 1.5 * stencil_weights[0] - center_level) * (1.0 / half_width)

    def fill(n, carry):
        for x in range(wx):
            tall[0, n, x, 8:16] = own[0, n, x]
        return carry

    lax.fori_loop(0, norb, fill, 0)
    heard(0)
    relay(1)
    run(0, 0, cut)
    heard(1)
    relay(2)
    run(1, 0, cut)
    run(-1, cut, chunks)
    heard(2)
    run(2, 0, cut - 1)
    run(0, cut, chunks)
    run(2, cut - 1, cut)
    run(3, 0, cut - 1)
    run(1, cut, chunks)
    run(3, cut - 1, cut)
    run(2, cut, chunks)
    save = pltpu.make_async_copy(own.at[3], filt_ref, load_sem.at[0])
    save.start()
    run(3, cut, chunks)

    def all_of(ref, count, send, recv, peer):
        part = ref.at[pl.ds(0, count)]
        return pltpu.make_async_remote_copy(
            src_ref=part, dst_ref=part, send_sem=send, recv_sem=recv, device_id=peer, device_id_type=MESH
        )

    def z_done(which):
        return all_of(gather.at[which], norb * wx * (nb - 1), z_send.at[which], z_recv.at[which], sides[4])

    def rows_done(which):
        return all_of(rows_in.at[which], nb - 1, r_send.at[which], r_recv.at[which], sides[4])

    def gx_done(which):
        return all_of(gx_in.at[which], ngx - 1, s_send.at[which, 0], s_recv.at[which, 0], sides[0])

    def gy_done(which):
        return all_of(gy_in.at[which], ngy - 1, s_send.at[which, 1], s_recv.at[which, 1], sides[2])

    def operand(which):
        return jnp.concatenate(
            [gather[which, pl.ds(x, total_orbs, stride=wx), :] for x in range(wx)], axis=1
        )

    def product(a, b):
        return lax.dot_general(
            a, b, (((1,), (1,)), ((), ())), precision=lax.Precision.HIGHEST, preferred_element_type=F32
        )

    def scatter(which, value):
        blocks = value.reshape(nb, norb, total_orbs)
        rows_out[which, :, 0:norb] = blocks[:, :, 0:128]
        tail[:, 0:norb, 0:32] = blocks[:, :, 128:160]
        for b in range(nb):
            packed = tail[b, 0:8] + pltpu.roll(tail[b, 8:16], 32, 1) + pltpu.roll(tail[b, 16:24], 64, 1)
            rows_out[which, b, 24:32] = packed
        rows_in[which, band] = rows_out[which, band]
        for d in (4, 3, -3, 2, -2, 1, -1):
            peer = lax.rem(band + d + nb, nb)
            pltpu.make_async_remote_copy(
                src_ref=rows_out.at[which, peer],
                dst_ref=rows_in.at[which, band],
                send_sem=r_send.at[which],
                recv_sem=r_recv.at[which],
                device_id={"band": peer},
                device_id_type=MESH,
            ).start()

    def ordered(ref, count):
        value = ref[0]
        for i in range(1, count):
            value = value + ref[i]
        return value

    def over_gx(which):
        rows_done(which).wait_recv()
        gx_in[which, gx] = ordered(rows_in.at[which], nb)
        for d in (4, 3, 5, 2, 6, 1, 7):
            pltpu.make_async_remote_copy(
                src_ref=gx_in.at[which, gx],
                dst_ref=gx_in.at[which, gx],
                send_sem=s_send.at[which, 0],
                recv_sem=s_recv.at[which, 0],
                device_id={"gx": lax.rem(gx + d, ngx)},
                device_id_type=MESH,
            ).start()

    def over_gy(which):
        gx_done(which).wait_recv()
        gy_in[which, gy] = ordered(gx_in.at[which], ngx)
        for d in (2, 1, 3):
            pltpu.make_async_remote_copy(
                src_ref=gy_in.at[which, gy],
                dst_ref=gy_in.at[which, gy],
                send_sem=s_send.at[which, 1],
                recv_sem=s_recv.at[which, 1],
                device_id={"gy": lax.rem(gy + d, ngy)},
                device_id_type=MESH,
            ).start()

    def finish(which):
        gy_done(which).wait_recv()
        sums_ref[which] = ordered(gy_in.at[which], ngy) * scale

    z_done(0).wait_recv()
    scatter(0, product(operand(0), operand(0)))
    z_done(1).wait_recv()
    one_way = product(operand(0), operand(1))
    scatter(1, one_way + one_way.T)
    over_gx(0)
    over_gy(0)
    over_gx(1)
    finish(0)
    over_gy(1)
    finish(1)

    for level in range(4):
        for side in range(4):
            halo_copy(level, 0, norb, 0, side).wait_send()
    for which in range(2):
        z_done(which).wait_send()
        rows_done(which).wait_send()
        gx_done(which).wait_send()
        gy_done(which).wait_send()
    save.wait()


def deliver(sums_ref, filt_ref, out_ref, corr_ref, proj_ref):
    out_ref[...] = filt_ref[...]
    norb = corr_ref.shape[0]
    for which, out in enumerate((corr_ref, proj_ref)):
        value = sums_ref[which]
        out[:, 0:128] = value[0:norb]
        rest = value[24:32]
        out[0:8, 128:160] = rest[:, 0:32]
        out[8:16, 128:160] = pltpu.roll(rest, 96, 1)[:, 0:32]
        out[16:20, 128:160] = pltpu.roll(rest, 64, 1)[0:4, 0:32]


def body(orbitals, potential):
    norb, wx, wy, nz = orbitals.shape
    ngx, ngy, nb = lax.axis_size("gx"), lax.axis_size("gy"), lax.axis_size("band")
    total = norb * nb
    chunks = norb // PART
    scale = 1.0 / (wx * wy * nz * ngx * ngy)
    block = (norb, wx, wy, nz)
    vmem = pl.BlockSpec(memory_space=pltpu.VMEM)
    hbm = pl.BlockSpec(memory_space=pltpu.HBM)
    filtered, sums = pl.pallas_call(
        functools.partial(kernel, (ngx, ngy, nb), scale),
        out_shape=(
            jax.ShapeDtypeStruct(block, F32),
            jax.ShapeDtypeStruct((2, 32, 128), F32),
        ),
        in_specs=[hbm, hbm],
        out_specs=(hbm, vmem),
        scratch_shapes=[
            pltpu.VMEM((5,) + block, F32),
            pltpu.VMEM((4, norb, wx, 24, nz), F32),
            pltpu.VMEM((4,) + block, F32),
            pltpu.VMEM((4,) + block, F32),
            pltpu.VMEM((wx, wy, nz), F32),
            pltpu.VMEM((12, wy, nz), F32),
            pltpu.VMEM((2, chunks, nb, PART * wx, nz), F32),
            pltpu.VMEM((2, total * wx, nz), F32),
            pltpu.VMEM((nb, 24, 128), F32),
            pltpu.VMEM((2, nb, 32, 128), F32),
            pltpu.VMEM((2, nb, 32, 128), F32),
            pltpu.VMEM((2, ngx, 32, 128), F32),
            pltpu.VMEM((2, ngy, 32, 128), F32),
            pltpu.SemaphoreType.DMA((2,)),
            pltpu.SemaphoreType.REGULAR((3,)),
            pltpu.SemaphoreType.DMA((4, 4)),
            pltpu.SemaphoreType.DMA((4, chunks, 4)),
            pltpu.SemaphoreType.DMA((2,)),
            pltpu.SemaphoreType.DMA((2,)),
            pltpu.SemaphoreType.DMA((2,)),
            pltpu.SemaphoreType.DMA((2,)),
            pltpu.SemaphoreType.DMA((2, 2)),
            pltpu.SemaphoreType.DMA((2, 2)),
        ],
        compiler_params=pltpu.CompilerParams(
            collective_id=0, has_side_effects=True, vmem_limit_bytes=60 * 1024 * 1024
        ),
        cost_estimate=pl.CostEstimate(flops=200_000_000, bytes_accessed=2_000_000, transcendentals=0),
    )(orbitals, potential)
    return pl.pallas_call(
        deliver,
        out_shape=(
            jax.ShapeDtypeStruct(block, F32),
            jax.ShapeDtypeStruct((norb, total), F32),
            jax.ShapeDtypeStruct((norb, total), F32),
        ),
        in_specs=[vmem, vmem],
        out_specs=(vmem, vmem, vmem),
        cost_estimate=pl.CostEstimate(flops=10_000, bytes_accessed=1_000_000, transcendentals=0),
    )(sums, filtered)


def solution(mesh):
    in_specs = (P("band", "gx", "gy", None), P("gx", "gy", None))
    out_specs = (P("band", "gx", "gy", None), P("band", None), P("band", None))
    return jax.shard_map(body, mesh=mesh, in_specs=in_specs, out_specs=out_specs, check_vma=False)
```

```python
import functools

import jax
import jax.numpy as jnp
from jax import lax
from jax.experimental import pallas as pl
from jax.experimental.pallas import tpu as pltpu
from jax.sharding import PartitionSpec as P

stencil_weights = (
    -5369.0 / 1800.0,
    12.0 / 7.0,
    -15.0 / 56.0,
    10.0 / 189.0,
    -1.0 / 112.0,
    2.0 / 1925.0,
    -1.0 / 16632.0,
)
center_level = 7.5
half_width = 4.5

MESH = pl.DeviceIdType.MESH
F32 = jnp.float32
PART = 4


def kernel(
    dims,
    scale,
    v_ref,
    pot_ref,
    filt_ref,
    sums_ref,
    own,
    tall,
    xlo,
    xhi,
    diag,
    shift_w,
    stage,
    gather,
    tail,
    rows_out,
    rows_in,
    gx_in,
    gy_in,
    load_sem,
    ready,
    halo_send,
    halo_recv,
    z_send,
    z_recv,
    r_send,
    r_recv,
    s_send,
    s_recv,
):
    ngx, ngy, nb = dims
    norb, wx, wy, nz = own.shape[1:]
    chunks = norb // PART
    total_orbs = norb * nb
    half_x, half_y = wx // 2, wy // 2
    gx, gy, band = lax.axis_index("gx"), lax.axis_index("gy"), lax.axis_index("band")

    load = pltpu.make_async_copy(v_ref, own.at[0], load_sem.at[0])
    load.start()
    load_pot = pltpu.make_async_copy(pot_ref, diag, load_sem.at[1])
    load_pot.start()

    sides = (
        {"gx": lax.rem(gx + 1, ngx)},
        {"gx": lax.rem(gx + ngx - 1, ngx)},
        {"gy": lax.rem(gy + 1, ngy)},
        {"gy": lax.rem(gy + ngy - 1, ngy)},
        {"band": lax.rem(band + 1, nb)},
        {"band": lax.rem(band + nb - 1, nb)},
    )

    barrier = pltpu.get_barrier_semaphore()
    for peer in sides:
        pl.semaphore_signal(barrier, 1, device_id=peer, device_id_type=MESH)

    def clear(n, carry):
        for x in range(wx):
            xlo[3, n, x, 0:half_y] = jnp.zeros((half_y, nz), F32)
            xhi[3, n, x, half_y:wy] = jnp.zeros((wy - half_y, nz), F32)
            if x < half_x:
                tall[3, n, x, 0:8] = jnp.zeros((8, nz), F32)
            else:
                tall[3, n, x, 16:24] = jnp.zeros((8, nz), F32)
        return carry

    lax.fori_loop(0, norb, clear, 0)

    taps = [0.0] + [-0.5 * w / half_width for w in stencil_weights[1:]]
    lane = lax.broadcasted_iota(jnp.int32, (wy, nz), 1)

    spots = (
        [(0, j) for j in (-2, -1, 1, 2)]
        + [(5, j) for j in (-2, -1, 0, 1)]
        + [(-5, j) for j in (-1, 0, 1, 2)]
    )
    for i, (far, j) in enumerate(spots):
        where = lane + far
        where = jnp.where(where >= nz, where - nz, jnp.where(where < 0, where + nz, where))
        source = where - (far + j)
        inside = jnp.logical_and(source >= 0, source < nz)
        shift_w[i] = jnp.where(inside, taps[abs(far + j)], 0.0)

    tail[...] = jnp.zeros_like(tail)
    load.wait()
    pl.semaphore_wait(barrier, 6)

    def relay(turn):
        for peer in sides[4:]:
            pl.semaphore_signal(ready.at[turn], 1, device_id=peer, device_id_type=MESH)

    def heard(turn):
        pl.semaphore_wait(ready.at[turn], 2)

    def halo_copy(level, start, count, sem_at, side):
        group = pl.ds(start, count)
        if level < 3:
            src = (
                own.at[level, group],
                own.at[level, group],
                own.at[level, group, :, 2:8],
                own.at[level, group, :, 0:6],
            )[side]
            dst = (
                xlo.at[level, group],
                xhi.at[level, group],
                tall.at[level, group, :, 2:8],
                tall.at[level, group, :, 16:22],
            )[side]
        else:
            src = (
                own.at[level, group, :, half_y:wy],
                own.at[level, group, :, 0:half_y],
                own.at[level, group, half_x:wx, 2:8],
                own.at[level, group, 0:half_x, 0:6],
            )[side]
            dst = (
                xlo.at[level, group, :, half_y:wy],
                xhi.at[level, group, :, 0:half_y],
                tall.at[level, group, half_x:wx, 2:8],
                tall.at[level, group, 0:half_x, 16:22],
            )[side]
        return pltpu.make_async_remote_copy(
            src_ref=src,
            dst_ref=dst,
            send_sem=halo_send.at[level, side],
            recv_sem=halo_recv.at[level, sem_at, side],
            device_id=sides[side],
            device_id_type=MESH,
        )

    def halo_start(level, c, which=(2, 3, 0, 1)):
        for side in which:
            halo_copy(level, c * PART, PART, c, side).start()

    def halo_wait(level, c):
        for side in (0, 1, 2, 3):
            halo_copy(level, c * PART, PART, c, side).wait_recv()

    def base(level, n):
        inner = [own[level, n, x] for x in range(wx)]
        if level == 3:
            inner = [0.5 * v for v in inner]
        line = [xlo[level, n, x] for x in range(wx)] + inner + [xhi[level, n, x] for x in range(wx)]
        out = []
        for x in range(wx):
            v = inner[x]
            total = diag[x] * v
            for k in range(1, 7):
                near = line[wx + x + k] + line[wx + x - k]
                near += tall[level, n, x, 8 + k : 16 + k] + tall[level, n, x, 8 - k : 16 - k]
                total += taps[k] * near
            rolled = {0: v}
            for j in (-2, -1, 1, 2):
                rolled[j] = pltpu.roll(v, j % nz, 1)
            parts = {0: None, 5: None, -5: None}
            for i, (far, j) in enumerate(spots):
                term = shift_w[i] * rolled[j]
                parts[far] = term if parts[far] is None else parts[far] + term
            total += parts[0]
            total += pltpu.roll(parts[5], 5, 1) + pltpu.roll(parts[-5], nz - 5, 1)
            out.append(total)
        return out

    def z_rows(c):
        return pl.ds(pl.multiple_of(band * (norb * wx) + c * (PART * wx), 8), PART * wx)

    def spread(which, c, value):
        stage[which, c] = jnp.swapaxes(value, 0, 1)
        gather[which, z_rows(c)] = stage[which, c, band]
        for d in (4, 3, -3, 2, -2, 1, -1):
            peer = lax.rem(band + d + nb, nb)
            pltpu.make_async_remote_copy(
                src_ref=stage.at[which, c, peer],
                dst_ref=gather.at[which, z_rows(c)],
                send_sem=z_send.at[which],
                recv_sem=z_recv.at[which],
                device_id={"band": peer},
                device_id_type=MESH,
            ).start()

    def step(level, c):
        halo_wait(level, c)

        def one(i, carry):
            n = c * PART + i
            for x, value in enumerate(base(level, n)):
                if level in (1, 2):
                    value = 2.0 * value - own[level - 1, n, x]
                elif level == 3:
                    value = half_width * value + (0.5 * center_level) * own[3, n, x]
                own[level + 1, n, x] = value
                if level < 3:
                    tall[level + 1, n, x, 8:16] = 0.5 * value if level == 2 else value
            return carry

        lax.fori_loop(0, PART, one, 0, unroll=4)
        if level < 3:
            halo_start(level + 1, c)
        if level >= 2:
            spread(level - 2, c, own[level + 1, pl.ds(c * PART, PART)].reshape(PART * wx, wy, nz))

    def run(level, first, end, which=(2, 3, 0, 1)):
        def body(c, carry):
            if level < 0:
                halo_start(0, c, which)
            else:
                step(level, c)
            return carry

        lax.fori_loop(first, end, body, 0)

    cut = (chunks + 1) // 2
    run(-1, 0, cut)
    relay(0)
    load_pot.wait()
    diag[...] = (diag[...] - 1.5 * stencil_weights[0] - center_level) * (1.0 / half_width)

    def fill(n, carry):
        for x in range(wx):
            tall[0, n, x, 8:16] = own[0, n, x]
        return carry

    lax.fori_loop(0, norb, fill, 0)
    heard(0)
    relay(1)
    run(0, 0, cut)
    heard(1)
    relay(2)
    run(1, 0, cut)
    run(-1, cut, chunks, (2, 3))
    run(-1, cut, chunks, (0, 1))
    heard(2)
    run(2, 0, cut - 1)
    run(0, cut, chunks)
    run(2, cut - 1, cut)
    run(3, 0, cut - 1)
    run(1, cut, chunks)
    run(3, cut - 1, cut)
    run(2, cut, chunks)
    save = pltpu.make_async_copy(own.at[3], filt_ref, load_sem.at[0])
    save.start()
    run(3, cut, chunks)

    def all_of(ref, count, send, recv, peer):
        part = ref.at[pl.ds(0, count)]
        return pltpu.make_async_remote_copy(
            src_ref=part, dst_ref=part, send_sem=send, recv_sem=recv, device_id=peer, device_id_type=MESH
        )

    def z_done(which):
        return all_of(gather.at[which], norb * wx * (nb - 1), z_send.at[which], z_recv.at[which], sides[4])

    def rows_done(which):
        return all_of(rows_in.at[which], nb - 1, r_send.at[which], r_recv.at[which], sides[4])

    def gx_done(which):
        return all_of(gx_in.at[which], ngx - 1, s_send.at[which, 0], s_recv.at[which, 0], sides[0])

    def gy_done(which):
        return all_of(gy_in.at[which], ngy - 1, s_send.at[which, 1], s_recv.at[which, 1], sides[2])

    def operand(which):
        return jnp.concatenate(
            [gather[which, pl.ds(x, total_orbs, stride=wx), :] for x in range(wx)], axis=1
        )

    def product(a, b):
        return lax.dot_general(
            a, b, (((1,), (1,)), ((), ())), precision=lax.Precision.HIGHEST, preferred_element_type=F32
        )

    def scatter(which, value):
        blocks = value.reshape(nb, norb, total_orbs)
        rows_out[which, :, 0:norb] = blocks[:, :, 0:128]
        tail[:, 0:norb, 0:32] = blocks[:, :, 128:160]
        for b in range(nb):
            packed = tail[b, 0:8] + pltpu.roll(tail[b, 8:16], 32, 1) + pltpu.roll(tail[b, 16:24], 64, 1)
            rows_out[which, b, 24:32] = packed
        rows_in[which, band] = rows_out[which, band]
        for d in (4, 3, -3, 2, -2, 1, -1):
            peer = lax.rem(band + d + nb, nb)
            pltpu.make_async_remote_copy(
                src_ref=rows_out.at[which, peer],
                dst_ref=rows_in.at[which, band],
                send_sem=r_send.at[which],
                recv_sem=r_recv.at[which],
                device_id={"band": peer},
                device_id_type=MESH,
            ).start()

    def ordered(ref, count):
        value = ref[0]
        for i in range(1, count):
            value = value + ref[i]
        return value

    def over_gx(which):
        rows_done(which).wait_recv()
        gx_in[which, gx] = ordered(rows_in.at[which], nb)
        for d in (4, 3, 5, 2, 6, 1, 7):
            pltpu.make_async_remote_copy(
                src_ref=gx_in.at[which, gx],
                dst_ref=gx_in.at[which, gx],
                send_sem=s_send.at[which, 0],
                recv_sem=s_recv.at[which, 0],
                device_id={"gx": lax.rem(gx + d, ngx)},
                device_id_type=MESH,
            ).start()

    def over_gy(which):
        gx_done(which).wait_recv()
        gy_in[which, gy] = ordered(gx_in.at[which], ngx)
        for d in (2, 1, 3):
            pltpu.make_async_remote_copy(
                src_ref=gy_in.at[which, gy],
                dst_ref=gy_in.at[which, gy],
                send_sem=s_send.at[which, 1],
                recv_sem=s_recv.at[which, 1],
                device_id={"gy": lax.rem(gy + d, ngy)},
                device_id_type=MESH,
            ).start()

    def finish(which):
        gy_done(which).wait_recv()
        sums_ref[which] = ordered(gy_in.at[which], ngy) * scale

    z_done(0).wait_recv()
    scatter(0, product(operand(0), operand(0)))
    z_done(1).wait_recv()
    one_way = product(operand(0), operand(1))
    scatter(1, one_way + one_way.T)
    over_gx(0)
    over_gy(0)
    over_gx(1)
    finish(0)
    over_gy(1)
    finish(1)

    for level in range(4):
        for side in range(4):
            halo_copy(level, 0, norb, 0, side).wait_send()
    for which in range(2):
        z_done(which).wait_send()
        rows_done(which).wait_send()
        gx_done(which).wait_send()
        gy_done(which).wait_send()
    save.wait()


def deliver(sums_ref, filt_ref, out_ref, corr_ref, proj_ref):
    out_ref[...] = filt_ref[...]
    norb = corr_ref.shape[0]
    for which, out in enumerate((corr_ref, proj_ref)):
        value = sums_ref[which]
        out[:, 0:128] = value[0:norb]
        rest = value[24:32]
        out[0:8, 128:160] = rest[:, 0:32]
        out[8:16, 128:160] = pltpu.roll(rest, 96, 1)[:, 0:32]
        out[16:20, 128:160] = pltpu.roll(rest, 64, 1)[0:4, 0:32]


def body(orbitals, potential):
    norb, wx, wy, nz = orbitals.shape
    ngx, ngy, nb = lax.axis_size("gx"), lax.axis_size("gy"), lax.axis_size("band")
    total = norb * nb
    chunks = norb // PART
    scale = 1.0 / (wx * wy * nz * ngx * ngy)
    block = (norb, wx, wy, nz)
    vmem = pl.BlockSpec(memory_space=pltpu.VMEM)
    hbm = pl.BlockSpec(memory_space=pltpu.HBM)
    filtered, sums = pl.pallas_call(
        functools.partial(kernel, (ngx, ngy, nb), scale),
        out_shape=(
            jax.ShapeDtypeStruct(block, F32),
            jax.ShapeDtypeStruct((2, 32, 128), F32),
        ),
        in_specs=[hbm, hbm],
        out_specs=(hbm, vmem),
        scratch_shapes=[
            pltpu.VMEM((5,) + block, F32),
            pltpu.VMEM((4, norb, wx, 24, nz), F32),
            pltpu.VMEM((4,) + block, F32),
            pltpu.VMEM((4,) + block, F32),
            pltpu.VMEM((wx, wy, nz), F32),
            pltpu.VMEM((12, wy, nz), F32),
            pltpu.VMEM((2, chunks, nb, PART * wx, nz), F32),
            pltpu.VMEM((2, total * wx, nz), F32),
            pltpu.VMEM((nb, 24, 128), F32),
            pltpu.VMEM((2, nb, 32, 128), F32),
            pltpu.VMEM((2, nb, 32, 128), F32),
            pltpu.VMEM((2, ngx, 32, 128), F32),
            pltpu.VMEM((2, ngy, 32, 128), F32),
            pltpu.SemaphoreType.DMA((2,)),
            pltpu.SemaphoreType.REGULAR((3,)),
            pltpu.SemaphoreType.DMA((4, 4)),
            pltpu.SemaphoreType.DMA((4, chunks, 4)),
            pltpu.SemaphoreType.DMA((2,)),
            pltpu.SemaphoreType.DMA((2,)),
            pltpu.SemaphoreType.DMA((2,)),
            pltpu.SemaphoreType.DMA((2,)),
            pltpu.SemaphoreType.DMA((2, 2)),
            pltpu.SemaphoreType.DMA((2, 2)),
        ],
        compiler_params=pltpu.CompilerParams(
            collective_id=0, has_side_effects=True, vmem_limit_bytes=60 * 1024 * 1024
        ),
        cost_estimate=pl.CostEstimate(flops=200_000_000, bytes_accessed=2_000_000, transcendentals=0),
    )(orbitals, potential)
    return pl.pallas_call(
        deliver,
        out_shape=(
            jax.ShapeDtypeStruct(block, F32),
            jax.ShapeDtypeStruct((norb, total), F32),
            jax.ShapeDtypeStruct((norb, total), F32),
        ),
        in_specs=[vmem, vmem],
        out_specs=(vmem, vmem, vmem),
        cost_estimate=pl.CostEstimate(flops=10_000, bytes_accessed=1_000_000, transcendentals=0),
    )(sums, filtered)


def solution(mesh):
    in_specs = (P("band", "gx", "gy", None), P("gx", "gy", None))
    out_specs = (P("band", "gx", "gy", None), P("band", None), P("band", None))
    return jax.shard_map(body, mesh=mesh, in_specs=in_specs, out_specs=out_specs, check_vma=False)
```
